512 devices in a mesh: layer: 16 (over z), tile: 32 (over x, y, core).
Axes of the slice: x: 4, y: 4, z: 16, core: 2. Of those that a mesh axis runs over, the one named last changes fastest.
Arguments:
- start: bfloat16 [16, 256, 8192], P(None, 'layer', 'tile'), may hold values from -2.6 to 2.6
- site_weight: float32 [256, 8192], P('layer', 'tile'), may hold values from 0.24 to 4.48, as said below
- onsite: float32 [256, 8192], P('layer', 'tile'), may hold values from -0.5 to 0.5
- hop_right: float32 [256, 8192], P('layer', 'tile'), may hold values from 0.6 to 1.2
- hop_down: float32 [256, 8192], P('layer', 'tile'), may hold values from 0.6 to 1.2
- send_rows: int32 [128, 128, 128], P('layer', 'tile'), may hold values from 0 to 4095
- recv_rows: int32 [128, 128, 128], P('layer', 'tile'), may hold values from 0 to 4095
- block_counts: int32 [128, 32], P('layer', 'tile'), may hold values from 0 to 4, as said below
- inter_blocks: bfloat16 [128, 128, 128, 128], P('layer', 'tile'), may hold values from -0.5 to 0.5
Outputs:
- final_panel: bfloat16 [32, 256, 8192], P(None, 'layer', 'tile')
- moments: float32 [4, 4], replicated
The draws below stay inside these ranges and needn't reach their ends.
Inputs may be any that keep to these rules, and one draw needn't show every extreme that they name: block_counts[i * 8 + l, t] is exactly 4 for l = i // 2, lies between 1 and 4 for l = i // 2 - 1 and l = i // 2 + 1, and is 0 for every other l: a device couples only to the device i xor 1 of the other layer and that device's two neighbours within its layer. `site_weight`: positive weights.
All inputs are finite; a program needn't handle non-finite values.
Results may differ from the reference program's by a relative error of at most 0.0034.
Values may be sent and summed in bfloat16 or wider, within the bound.
No kernel may reach another device: no remote copies, remote signals or barrier semaphores. Data moves between devices by JAX's collectives and lax.ppermute only.
A program may use at most 64 MiB of HBM per device.

```python
import jax
import jax.numpy as jnp
from jax import lax

NVEC = 16
GX = 16
GY = 256
NB = 4
BLK = 128
ORDER = 4
HALF = 8
SITES = 4096
XTOT = 256
YTOT = 8192
N_LAYER = 16
N_TILE = 32


def draw_start(key, part):
    vector_place = jnp.arange(NVEC, dtype=jnp.float32) / (NVEC - 1)
    levels = 0.15 * jnp.power(10.0, vector_place)
    values = jax.random.uniform(key, (NVEC, XTOT, YTOT), jnp.float32, -1.7, 1.7)
    return (levels[:, None, None] * values).astype(jnp.bfloat16)


def draw_site_weight(key, part):
    roughness = jax.random.uniform(key, (XTOT, YTOT), jnp.float32, 0.6, 1.4)
    row_place = jnp.arange(XTOT, dtype=jnp.float32)[:, None] / XTOT
    col_place = jnp.arange(YTOT, dtype=jnp.float32)[None, :] / YTOT
    col_number = jnp.arange(YTOT, dtype=jnp.int32)[None, :]
    contrast = jnp.where(col_number % 2 == 0, 1.6, 0.4).astype(jnp.float32)
    return contrast * (1.0 + 0.5 * (row_place + col_place)) * roughness


def draw_block_counts(key, part):
    first_key = jax.random.fold_in(key, 11)
    base_counts = jax.random.randint(first_key, (N_LAYER, HALF, N_TILE), 1, NB + 1)
    device_index = lax.broadcasted_iota(jnp.int32, (N_LAYER, HALF, N_TILE), 0)
    slot_index = lax.broadcasted_iota(jnp.int32, (N_LAYER, HALF, N_TILE), 1)
    offset = slot_index - device_index // 2
    near_counts = jnp.where(jnp.abs(offset) == 1, base_counts, jnp.zeros_like(base_counts))
    full_counts = jnp.where(offset == 0, jnp.full_like(base_counts, NB), near_counts)
    return full_counts.reshape(N_LAYER * HALF, N_TILE).astype(jnp.int32)


def touch_ends(result, key, smallest, largest):
    longest = result.shape.index(max(result.shape))
    spots = []
    for shift in (0, 1):
        where = [jax.random.randint(jax.random.fold_in(key, axis), (), 0, length) for axis, length in enumerate(result.shape)]
        where[longest] = (where[longest] + shift) % result.shape[longest]
        spots.append(tuple(where))
    return result.at[spots[0]].set(smallest).at[spots[1]].set(largest)


def shard_levels(rng, shape, pieces, smallest, high):
    factor_of = 1.0
    for dim, blocks in pieces:
        steps = jax.random.uniform(jax.random.fold_in(jax.random.fold_in(rng, 6), dim), (blocks,), jnp.float32, smallest / len(pieces), high / len(pieces))
        factor_of = factor_of * jnp.repeat(jnp.exp(steps), shape[dim] // blocks).reshape((-1,) + (1,) * (len(shape) - 1 - dim))
    return factor_of


def bell_draw(stream_key, shape, deviation, limit, split=(), held_as=jnp.bfloat16):
    loudness = shard_levels(stream_key, shape, split, -0.22, 0.18) if split else 1.0
    drawn = jax.random.normal(stream_key, shape, jnp.float32) * deviation * loudness
    return jnp.minimum(jnp.maximum(drawn, -limit), limit).astype(held_as)


def setup_inputs(seed: int = 0) -> dict:
    arg_keys = jax.random.split(jax.random.key(seed), 10)
    return {
        "start": draw_start(jax.random.fold_in(arg_keys[9], 71), 0),
        "site_weight": draw_site_weight(jax.random.fold_in(arg_keys[9], 71), 0),
        "onsite": jnp.clip(jax.random.uniform(arg_keys[2], (XTOT, YTOT), jnp.float32, -0.5, 0.5) * shard_levels(arg_keys[2], (XTOT, YTOT), ((0, 16), (1, 32)), -0.4, 0.0), -0.5, 0.5),
        "hop_right": jnp.clip(0.6 + 0.6 * jax.random.uniform(arg_keys[3], (XTOT, YTOT), jnp.float32) ** shard_levels(arg_keys[3], (XTOT, YTOT), ((0, 16), (1, 32)), -0.2, 0.2), 0.6, 1.2),
        "hop_down": jnp.clip(0.6 + 0.6 * jax.random.uniform(arg_keys[4], (XTOT, YTOT), jnp.float32) ** shard_levels(arg_keys[4], (XTOT, YTOT), ((0, 16), (1, 32)), -0.2, 0.2), 0.6, 1.2),
        "send_rows": touch_ends(jax.random.randint(arg_keys[5], (N_LAYER * HALF, N_TILE * NB, BLK), 0, SITES), jax.random.fold_in(arg_keys[5], 1), 0, SITES - 1).astype(jnp.int32),
        "recv_rows": touch_ends(jax.random.randint(arg_keys[6], (N_LAYER * HALF, N_TILE * NB, BLK), 0, SITES), jax.random.fold_in(arg_keys[6], 1), 0, SITES - 1).astype(jnp.int32),
        "block_counts": draw_block_counts(jax.random.fold_in(arg_keys[9], 71), 0),
        "inter_blocks": bell_draw(arg_keys[8], (N_LAYER * HALF, N_TILE * NB, BLK, BLK), BLK ** -0.5, 0.5, ((0, 16), (1, 32))),
    }


def neighbour(values, along, offset):
    extent = values.shape[along]
    zero_shape = list(values.shape)
    zero_shape[along] = 1
    padding = jnp.zeros(tuple(zero_shape), values.dtype)
    if offset > 0:
        return jnp.concatenate([lax.slice_in_dim(values, 1, extent, axis=along), padding], axis=along)
    return jnp.concatenate([padding, lax.slice_in_dim(values, 0, extent - 1, axis=along)], axis=along)


def panel_layers(vectors):
    count = vectors.shape[0]
    shaped = vectors.reshape(count, HALF, 2, GX, YTOT).transpose(2, 0, 1, 3, 4)
    return shaped.reshape(2, count, HALF * GX, YTOT)


def panel_grid(layered):
    count = layered.shape[1]
    shaped = layered.reshape(2, count, HALF, GX, YTOT).transpose(1, 2, 0, 3, 4)
    return shaped.reshape(count, XTOT, YTOT)


def field_layers(field):
    shaped = field.reshape(HALF, 2, GX, YTOT).transpose(1, 0, 2, 3)
    return shaped.reshape(2, 1, HALF * GX, YTOT)


def local_terms(vectors, onsite, hop_right, hop_left, bond_down, bond_up):
    right_cells = neighbour(vectors, 3, 1)
    left_cells = neighbour(vectors, 3, -1)
    lower_cells = neighbour(vectors, 2, 1)
    upper_cells = neighbour(vectors, 2, -1)
    along_chain = hop_right * right_cells - hop_left * left_cells
    in_layer = onsite * vectors - hop_right * right_cells - hop_left * left_cells - bond_down * lower_cells - bond_up * upper_cells
    return in_layer, along_chain


def device_blocks(vectors):
    panel_rows = vectors.shape[0]
    shaped = vectors.reshape(panel_rows, N_LAYER, GX, N_TILE, GY).transpose(1, 3, 0, 2, 4)
    return shaped.reshape(N_LAYER, N_TILE, panel_rows, GX * GY)


def device_lists(table):
    shaped = table.reshape(N_LAYER, HALF, N_TILE, NB, BLK).transpose(0, 2, 1, 3, 4)
    return shaped.reshape(N_LAYER, N_TILE, HALF * NB * BLK).astype(jnp.int32)


def cross_term(vectors, send_rows, recv_rows, block_counts, inter_blocks):
    panel_rows = vectors.shape[0]
    per_device = device_blocks(vectors)
    sources = device_lists(send_rows)
    targets = device_lists(recv_rows)

    def select_rows(device_values, device_rows):
        return jnp.take(device_values, device_rows, axis=1)

    selected = jax.vmap(jax.vmap(select_rows))(per_device, sources)
    live_counts = block_counts.reshape(N_LAYER, HALF, N_TILE).transpose(0, 2, 1).astype(jnp.int32)
    slot_ids = jnp.arange(NB, dtype=jnp.int32)[None, None, None, :]
    live_mask = (slot_ids < live_counts[:, :, :, None]).astype(jnp.bfloat16)
    outgoing = selected.astype(jnp.bfloat16).reshape(N_LAYER, N_TILE, panel_rows, HALF, NB, BLK)
    outgoing = outgoing * live_mask[:, :, None, :, :, None]
    by_side = outgoing.reshape(HALF, 2, N_TILE, panel_rows, HALF, NB, BLK)[:, ::-1]
    incoming = by_side.transpose(4, 1, 2, 3, 0, 5, 6).reshape(N_LAYER, N_TILE, panel_rows, HALF, NB, BLK)
    couplings = inter_blocks.reshape(N_LAYER, HALF, N_TILE, NB, BLK, BLK).transpose(0, 2, 1, 3, 4, 5)
    products = jnp.einsum("ltpabk,ltabkq->ltpabq", incoming.astype(jnp.float32), couplings.astype(jnp.float32))
    products = products.reshape(N_LAYER, N_TILE, panel_rows, HALF * NB * BLK)

    def place_rows(device_products, device_rows):
        return jnp.zeros((panel_rows, GX * GY), jnp.float32).at[:, device_rows].add(device_products)

    collected = jax.vmap(jax.vmap(place_rows))(products, targets)
    collected = collected.reshape(N_LAYER, N_TILE, panel_rows, GX, GY).transpose(2, 0, 3, 1, 4)
    return collected.reshape(panel_rows, XTOT, YTOT)


def reference(start, site_weight, onsite, hop_right, hop_down, send_rows, recv_rows, block_counts, inter_blocks):
    onsite_l = field_layers(onsite)
    right_l = field_layers(hop_right)
    down_l = field_layers(hop_down)
    row_index = jnp.arange(HALF * GX, dtype=jnp.int32)[None, None, :, None]
    col_index = jnp.arange(YTOT, dtype=jnp.int32)[None, None, None, :]
    parity_even = (row_index + col_index) % 2 == 0
    inside_half = row_index != HALF * GX - 1
    bond_down = jnp.where(jnp.logical_and(parity_even, inside_half), down_l, jnp.zeros_like(down_l))
    hop_left = neighbour(right_l, 3, -1)
    bond_up = neighbour(bond_down, 2, -1)
    right_start = panel_layers(site_weight[None] * start.astype(jnp.float32))
    left_start = local_terms(right_start, onsite_l, right_l, hop_left, bond_down, bond_up)[1]
    vectors = jnp.concatenate([left_start, right_start], axis=1)
    previous = vectors
    left_chain = []
    velocities = []
    for order_step in range(ORDER):
        in_layer, along_chain = local_terms(vectors, onsite_l, right_l, hop_left, bond_down, bond_up)
        left_chain.append(vectors[:, :NVEC])
        velocities.append(along_chain[:, NVEC:])
        crossing = panel_layers(cross_term(panel_grid(vectors), send_rows, recv_rows, block_counts, inter_blocks))
        applied = 0.25 * (in_layer + crossing)
        if order_step == 0:
            advanced = applied
        else:
            advanced = 2.0 * applied - previous
        previous = vectors
        vectors = advanced
    scale_factor = -0.25 / (NVEC * XTOT * YTOT)
    moment_rows = []
    for first_index in range(ORDER):
        moment_rows.append(jnp.stack([jnp.sum(left_chain[first_index] * velocities[second_index]) for second_index in range(ORDER)]))
    moments = jnp.stack(moment_rows) * scale_factor
    return panel_grid(vectors).astype(jnp.bfloat16), moments
```

```python
import functools

import jax
import jax.numpy as jnp
from jax import lax
from jax.experimental import pallas as pl
from jax.experimental.pallas import tpu as pltpu
from jax.sharding import PartitionSpec as P

ORDER = 4
F32 = jnp.float32
BF16 = jnp.bfloat16
NT = (((1,), (1,)), ((), ()))
TN = (((0,), (0,)), ((), ()))


def dot(a, b, dims=(((1,), (0,)), ((), ()))):
    return lax.dot_general(a, b, dims, preferred_element_type=F32)


def call(body, outs, scratch=(), scalars=1):
    def run(*args):
        specs = [
            pl.BlockSpec(memory_space=pltpu.SMEM if i < scalars else pltpu.VMEM)
            for i in range(len(args))
        ]
        return pl.pallas_call(
            body,
            out_shape=outs,
            in_specs=specs,
            out_specs=jax.tree.map(lambda _: pl.BlockSpec(memory_space=pltpu.VMEM), outs),
            scratch_shapes=list(scratch),
            compiler_params=pltpu.CompilerParams(vmem_limit_bytes=24 * 1024 * 1024),
        )(*args)

    return run


def unit_rows(places, breadth, rows=16):
    row = lax.broadcasted_iota(jnp.int32, (rows, breadth), 0)
    col = lax.broadcasted_iota(jnp.int32, (rows, breadth), 1)
    hit = jnp.zeros((rows, breadth), F32)
    for r, place in places.items():
        hit = jnp.where(jnp.logical_and(row == r, col == place), 1.0, hit)
    return hit.astype(BF16)


def rim_columns(info_ref, breadth):
    even = info_ref[0] == 0
    core = jnp.where(even, breadth - 1, 0)
    other = jnp.where(even, 0, breadth - 1)
    return core, other


def bonds(hop_down_ref, x):
    row = hop_down_ref[x : x + 1, :]
    col = lax.broadcasted_iota(jnp.int32, row.shape, 1)
    return jnp.where((col + x) % 2 == 0, row, 0.0)


def one_hot_columns(row, height):
    wide = lax.broadcasted_iota(jnp.int32, (height, row.shape[1]), 0)
    return jnp.where(wide == row, 1.0, 0.0).astype(BF16)


def sides(cells, rim):
    breadth = cells.shape[1]
    col = lax.broadcasted_iota(jnp.int32, cells.shape, 1)
    right = jnp.where(col == breadth - 1, rim, pltpu.roll(cells, breadth - 1, 1))
    left = jnp.where(col == 0, rim, pltpu.roll(cells, 1, 1))
    return right, left


def pre_body(info_ref, start_ref, weight_ref, hop_ref, core_ref, other_ref):
    height, count, breadth = start_ref.shape
    even = info_ref[0] == 0
    value, ahead, behind, hop_hi, hop_lo = [], [], [], [], []
    for x in range(height):
        right = weight_ref[x : x + 1, :] * start_ref[x].astype(F32)
        hop = jnp.broadcast_to(hop_ref[x : x + 1, :], right.shape)
        value.append(right.astype(BF16))
        ahead.append((hop * pltpu.roll(right, breadth - 1, 1)).astype(BF16))
        behind.append((hop * right).astype(BF16))
        hi = hop.astype(BF16)
        hop_hi.append(hi)
        hop_lo.append((hop - hi.astype(F32)).astype(BF16))
    value, ahead, behind, hop_hi, hop_lo = (
        jnp.concatenate(part, axis=0) for part in (value, ahead, behind, hop_hi, hop_lo)
    )
    last = breadth - 1
    to_left = dot(unit_rows({0: 0}, breadth), value, NT) + dot(
        unit_rows({1: 0}, breadth), ahead, NT
    )
    to_right = (
        dot(unit_rows({0: last}, breadth), value, NT)
        + dot(unit_rows({1: last - 1}, breadth), behind, NT)
        + dot(unit_rows({2: last}, breadth), hop_hi, NT)
        + dot(unit_rows({3: last}, breadth), hop_lo, NT)
    )
    core_ref[...] = jnp.where(even, to_right, to_left).astype(BF16)
    other_ref[...] = jnp.where(even, to_left, to_right).astype(BF16)


def gather_out(cells_ref, index_ref, out_ref):
    height, count, breadth = cells_ref.shape
    flat = cells_ref[...].reshape(height * count, breadth)
    for begin in range(0, index_ref.shape[1], 256):
        span = slice(begin, begin + 256)
        picked = dot(flat, one_hot_columns(index_ref[1:2, span], breadth))
        which = index_ref[0:1, span]
        total = jnp.zeros((count, 256), F32)
        for x in range(height):
            total = total + jnp.where(which == x, picked[x * count : (x + 1) * count], 0.0)
        out_ref[:, span] = total.astype(BF16)


def y_terms(x, cells, rim, above, below, fields):
    onsite_ref, hop_ref, left_ref, hop_down_ref = fields
    right, left = sides(cells, rim)
    flow_right = hop_ref[x : x + 1, :] * right
    flow_left = left_ref[x : x + 1, :] * left
    term = onsite_ref[x : x + 1, :] * cells - flow_right - flow_left
    if below is not None:
        term = term - bonds(hop_down_ref, x) * below
    if above is not None:
        term = term - bonds(hop_down_ref, x - 1) * above
    half = cells.shape[0] // 2
    return term, flow_right[half:] - flow_left[half:]


def init_body(
    info_ref,
    start_ref,
    weight_ref,
    onsite_ref,
    hop_ref,
    hop_down_ref,
    core_ref,
    other_ref,
    index_ref,
    panel_ref,
    left_ref,
    term_ref,
    flow_ref,
    out_ref,
    up_ref,
    down_ref,
    cells_ref,
):
    height, count, breadth = start_ref.shape
    core, other = rim_columns(info_ref, breadth)
    inner = info_ref[1].astype(F32)
    core_rows, other_rows = core_ref[...], other_ref[...]

    def spread(row):
        wide = dot(core_rows, unit_rows({row: core}, breadth), TN) + dot(
            other_rows, unit_rows({row: other}, breadth), TN
        )
        return wide.reshape(height, count, breadth)

    rim_right = spread(0)
    rim_part = spread(1)
    first = unit_rows({2: 0, 3: 0}, breadth)
    hop_first = (dot(core_rows, first, TN) + dot(other_rows, first, TN)).reshape(
        height, count, breadth
    )
    col = lax.broadcasted_iota(jnp.int32, (count, breadth), 1)
    rims = []
    for x in range(height):
        right_cells = weight_ref[x : x + 1, :] * start_ref[x].astype(F32)
        hop = hop_ref[x : x + 1, :]
        entry = hop_first[x][0:1, :]
        hop_left = jnp.where(col[0:1] == 0, entry, pltpu.roll(jnp.broadcast_to(hop, (8, breadth)), 1, 1)[0:1])
        left_ref[x : x + 1, :] = hop_left
        right, left = sides(right_cells, rim_right[x])
        left_cells = hop * right - hop_left * left
        rim_left = jnp.where(
            col == breadth - 1,
            inner * (rim_part[x] - hop * right_cells),
            jnp.where(col == 0, hop_left * right_cells - rim_part[x], 0.0),
        )
        rims.append(jnp.concatenate([rim_left, rim_right[x]], axis=0))
        cells = jnp.concatenate([left_cells, right_cells], axis=0)
        panel_ref[x] = cells
        cells_ref[x] = cells.astype(BF16)
    gather_out(cells_ref, index_ref, out_ref)
    up_ref[:, :breadth] = cells_ref[height - 1]
    down_ref[...] = cells_ref[0]
    last = bonds(hop_down_ref, height - 1)
    hi = last.astype(BF16).astype(F32)
    row = lax.broadcasted_iota(jnp.int32, (2 * count, breadth), 0)
    extra = jnp.where(row == 0, hi, jnp.where(row == 1, last - hi, 0.0))
    up_ref[:, breadth:] = extra.astype(BF16)
    fields = (onsite_ref, hop_ref, left_ref, hop_down_ref)
    for x in range(height):
        above = panel_ref[x - 1] if x > 0 else None
        below = panel_ref[x + 1] if x < height - 1 else None
        term, flow = y_terms(x, panel_ref[x], rims[x], above, below, fields)
        term_ref[x] = term
        flow_ref[x] = flow


def near_body(
    info_ref, panel_ref, onsite_ref, hop_ref, left_ref, hop_down_ref, core_ref, other_ref,
    term_ref, flow_ref,
):
    height, count, breadth = panel_ref.shape
    core, other = rim_columns(info_ref, breadth)
    rims = dot(core_ref[...], unit_rows({0: core}, breadth), TN) + dot(
        other_ref[...], unit_rows({0: other}, breadth), TN
    )
    fields = (onsite_ref, hop_ref, left_ref, hop_down_ref)
    for x in range(height):
        above = panel_ref[x - 1] if x > 0 else None
        below = panel_ref[x + 1] if x < height - 1 else None
        rim = rims[x * count : (x + 1) * count]
        term, flow = y_terms(x, panel_ref[x], rim, above, below, fields)
        term_ref[x] = term
        flow_ref[x] = flow


def moment_body(*refs):
    panels, flows, out_ref = refs[:ORDER], refs[ORDER : 2 * ORDER], refs[2 * ORDER]
    height, count, breadth = flows[0].shape
    totals = {}
    for x in range(height):
        lefts = [p[x, 0:count, :] for p in panels]
        rights = [f[x] for f in flows]
        for m in range(ORDER):
            for n in range(ORDER):
                term = lefts[m] * rights[n]
                part = term[:, 0:128]
                for begin in range(128, breadth, 128):
                    part = part + term[:, begin : begin + 128]
                folded = part[0:8]
                for begin in range(8, count, 8):
                    folded = folded + part[begin : begin + 8]
                totals[m, n] = folded + totals[m, n] if x else folded
    for m in range(ORDER):
        for n in range(ORDER):
            place = m * ORDER + n
            out_ref[place : place + 1, :] = jnp.sum(totals[m, n], axis=0, keepdims=True)


def far_body(
    step,
    info_ref,
    term_ref,
    prev_ref,
    partner_ref,
    above_ref,
    below_ref,
    bond_ref,
    hop_down_ref,
    blocks_ref,
    index_ref,
    *rest,
):
    last_step = step == ORDER - 1
    if last_step:
        final_ref, lhs_ref, = rest
    else:
        panel_ref, out_ref, core_ref, other_ref, up_ref, down_ref, lhs_ref, cells_ref = rest
    height, count, breadth = term_ref.shape
    total_span = index_ref.shape[1]
    part_span = total_span // 3
    blk = blocks_ref.shape[1]
    for d in range(3):
        for b in range(part_span // blk):
            begin = b * blk
            if d == 0:
                arriving = above_ref[:, begin : begin + blk]
            elif d == 1:
                arriving = partner_ref[:, part_span + begin : part_span + begin + blk]
            else:
                arriving = below_ref[:, begin : begin + blk]
            product = dot(arriving, blocks_ref[d * (part_span // blk) + b])
            place = d * part_span + begin
            which = index_ref[2:3, place : place + blk]
            for x in range(height):
                lhs_ref[x, :, place : place + blk] = jnp.where(which == x, product, 0.0).astype(BF16)
    targets = one_hot_columns(index_ref[3:4, :], breadth)
    crossing = dot(lhs_ref[...].reshape(height * count, total_span), targets, NT)
    bond_up = bond_ref[0:1, part_span + breadth :].astype(F32) + bond_ref[
        1:2, part_span + breadth :
    ].astype(F32)
    for x in range(height):
        term = term_ref[x] + crossing[x * count : (x + 1) * count]
        if x == 0:
            term = term - bond_up * above_ref[:, part_span : part_span + breadth].astype(F32)
        if x == height - 1:
            term = term - bonds(hop_down_ref, x) * below_ref[
                :, part_span : part_span + breadth
            ].astype(F32)
        if step == 0:
            cells = 0.25 * term
        else:
            cells = 0.5 * term - prev_ref[x]
        if last_step:
            final_ref[x] = cells.astype(BF16)
        else:
            panel_ref[x] = cells
            cells_ref[x] = cells.astype(BF16)
    if last_step:
        return
    gather_out(cells_ref, index_ref, out_ref)
    core, other = rim_columns(info_ref, breadth)
    flat = cells_ref[...].reshape(height * count, breadth)
    core_ref[...] = dot(unit_rows({0: core}, breadth), flat, NT).astype(BF16)
    other_ref[...] = dot(unit_rows({0: other}, breadth), flat, NT).astype(BF16)
    up_ref[...] = cells_ref[height - 1]
    down_ref[...] = cells_ref[0]


def shifted(x, axis, by):
    peers = lax.axis_size(axis)
    pairs = [(i, i + by) for i in range(peers) if 0 <= i + by < peers]
    return lax.ppermute(x, axis, pairs)


def tile_swaps(core, other):
    peers = lax.axis_size("tile")
    got_core = lax.ppermute(core, "tile", [(i, i ^ 1) for i in range(peers)])
    pairs = []
    for i in range(1, peers - 1, 2):
        pairs += [(i, i + 1), (i + 1, i)]
    return got_core, lax.ppermute(other, "tile", pairs)


def layer_exchange(outgoing, up, down):
    peers = lax.axis_size("layer")
    span = outgoing.shape[1] // 3
    partner = lax.ppermute(outgoing, "layer", [(i, i ^ 1) for i in range(peers)])
    above = shifted(jnp.concatenate([partner[:, 2 * span :], up], axis=1), "layer", 2)
    below = shifted(jnp.concatenate([partner[:, :span], down], axis=1), "layer", -2)
    return partner, above, below


def axis_total(x, axis):
    peers = lax.axis_size(axis)
    copies = jnp.broadcast_to(x[None], (peers,) + x.shape)
    return jnp.sum(lax.all_to_all(copies, axis, 0, 0), axis=0)


def local(start, site_weight, onsite, hop_right, hop_down, send_rows, recv_rows, block_counts, inter_blocks):
    count, height, breadth = start.shape
    half, slots, blk = send_rows.shape
    span = 3 * slots * blk
    lower = lax.axis_index("layer") // 2
    tile = lax.axis_index("tile")
    tiles = lax.axis_size("tile")
    info = jnp.stack([tile % 2, (tile != tiles - 1).astype(jnp.int32)])

    def near(table):
        wide = jnp.pad(table, ((1, 1), (0, 0), (0, 0)))
        return lax.dynamic_slice_in_dim(wide, lower, 3, axis=0)

    live = lax.broadcasted_iota(jnp.int32, send_rows.shape, 1) < block_counts[:, :, None]
    sends = near(jnp.where(live, send_rows, -breadth)).reshape(span)
    offset = lower + jnp.arange(3, dtype=jnp.int32)[:, None, None]
    inside = jnp.logical_and(offset > 0, offset <= half)
    sends = jnp.where(
        jnp.broadcast_to(inside, (3, slots, blk)).reshape(span), sends, -breadth
    )
    recvs = near(recv_rows).reshape(span)
    index = jnp.stack([sends // breadth, sends % breadth, recvs // breadth, recvs % breadth])
    index = jnp.concatenate([index, jnp.zeros((4, span), jnp.int32)], axis=0)
    blocks = jnp.concatenate(
        [
            lax.dynamic_index_in_dim(inter_blocks, jnp.clip(lower + d, 0, half - 1), 0, False)
            for d in (-1, 0, 1)
        ],
        axis=0,
    )
    turned = start.transpose(1, 0, 2)

    def of(shape, dtype=F32):
        return jax.ShapeDtypeStruct(shape, dtype)

    rim0 = of((16, height * count), BF16)
    core, other = call(pre_body, (rim0, rim0))(info, turned, site_weight, hop_right)
    core, other = tile_swaps(core, other)
    state = of((height, 2 * count, breadth))
    flow_shape = of((height, count, breadth))
    outgoing_shape = of((2 * count, span), BF16)
    face = of((2 * count, breadth), BF16)
    cells_scratch = pltpu.VMEM((height, 2 * count, breadth), BF16)
    lhs_scratch = pltpu.VMEM((height, 2 * count, span), BF16)
    panel, hop_left, term, flow, outgoing, up, down = call(
        init_body,
        (
            state,
            of((height, breadth)),
            state,
            flow_shape,
            outgoing_shape,
            of((2 * count, 2 * breadth), BF16),
            face,
        ),
        (cells_scratch,),
    )(info, turned, site_weight, onsite, hop_right, hop_down, core, other, index)
    panels, flows = [panel], [flow]
    bond_rows = None
    rim = of((16, height * 2 * count), BF16)
    for step in range(ORDER):
        partner, above, below = layer_exchange(outgoing, up, down)
        if step > 0:
            core, other = tile_swaps(core, other)
            term, flow = call(near_body, (state, flow_shape))(
                info, panels[-1], onsite, hop_right, hop_left, hop_down, core, other
            )
            flows.append(flow)
        if bond_rows is None:
            bond_rows = above
        previous = panels[-2] if step else panels[-1]
        args = (info, term, previous, partner, above, below, bond_rows, hop_down, blocks, index)
        if step < ORDER - 1:
            panel, outgoing, core, other, up, down = call(
                functools.partial(far_body, step),
                (state, outgoing_shape, rim, rim, face, face),
                (lhs_scratch, cells_scratch),
            )(*args)
            panels.append(panel)
        else:
            moments = call(moment_body, of((ORDER * ORDER, 128)), scalars=0)(*panels, *flows)
            moments = axis_total(axis_total(moments, "tile"), "layer")
            final = call(
                functools.partial(far_body, step),
                of((height, 2 * count, breadth), BF16),
                (lhs_scratch,),
            )(*args)
    cells = count * height * breadth * lax.axis_size("layer") * tiles
    moments = jnp.sum(moments, axis=1).reshape(ORDER, ORDER) * (-0.25 / cells)
    return final.transpose(1, 0, 2), moments


def solution(mesh):
    return jax.shard_map(
        local,
        mesh=mesh,
        in_specs=(
            P(None, "layer", "tile"),
            P("layer", "tile"),
            P("layer", "tile"),
            P("layer", "tile"),
            P("layer", "tile"),
            P("layer", "tile", None),
            P("layer", "tile", None),
            P("layer", "tile"),
            P("layer", "tile", None, None),
        ),
        out_specs=(P(None, "layer", "tile"), P()),
        check_vma=False,
    )
```
